32 devices in a mesh: groups: 2 (over y), dp: 4 (over z), tensor: 4 (over x, core).
Axes of the slice: x: 2, y: 2, z: 4, core: 2. Of those that a mesh axis runs over, the one named last changes fastest.
Arguments:
- normed_layer_input: bfloat16 [4096, 8192], P(('groups', 'dp'), 'tensor'), parts along dimension 0, may hold values from -6 to 6
- key_value_gradient: bfloat16 [4096, 2048], P(('groups', 'dp'), 'tensor'), parts along dimension 0, may hold values from -6 to 6
- key_value_weight: bfloat16 [8192, 2048], P(None, 'tensor'), may hold values from -0.0625 to 0.0625
- adapter_down_weight: bfloat16 [8, 16, 8192], P('dp', None, 'tensor'), may hold values from -0.0625 to 0.0625
- adapter_up_weight: bfloat16 [8, 16, 2048], P('dp', None, 'tensor'), may hold values from -1.5 to 1.5
- segment_adapter: int32 [32], P(('groups', 'dp')), parts along dimension 0, may hold values from 0 to 7
- slot_per_adapter: int32 [8], replicated, may hold values from 0 to 7, each once
Outputs:
- grad_input: bfloat16 [4096, 8192], P(('groups', 'dp'), 'tensor'), parts along dimension 0
- grad_down: float32 [16, 16, 8192], P(('groups', 'dp'), None, 'tensor'), parts along dimension 0
- grad_up: float32 [16, 16, 2048], P(('groups', 'dp'), None, 'tensor'), parts along dimension 0
The draws below stay inside these ranges and needn't reach their ends.
There are 2 independent parts, one for each index of `groups`. The reference program is written for one: setup_inputs(seed, part) draws one part's arguments, and reference() takes and returns one part's arrays. A program takes and returns all parts, laid end to end along the dimension named above; an argument that names none is the same for every part. Nothing has to cross between parts.
Inputs may be any that keep to these rules, and one draw needn't show every extreme that they name: `slot_per_adapter`: every slot once.
All inputs are finite; a program needn't handle non-finite values.
Results may differ from the reference program's by a relative error of at most 0.0046.
Values may be sent and summed in bfloat16 or wider, within the bound.
A program may use at most 128 MiB of HBM per device.

```python
import math
import jax
import jax.numpy as jnp
import numpy as np
from jax import lax

MODEL_WIDTH = 8192
KEY_VALUE_WIDTH = 1024
ADAPTER_RANK = 16
SEG = 128
ADAPTER_TOTAL = 8
SEGMENTS = 16
TOKENS = 2048


def plant(result, rng, smallest, high):
    dims = result.shape
    place = [jax.random.randint(jax.random.fold_in(rng, axis), (), 0, dims[axis]) for axis in range(len(dims))]
    result = result.at[tuple(place)].set(smallest)
    longest = dims.index(max(dims))
    place[longest] = (place[longest] + 1) % dims[longest]
    return result.at[tuple(place)].set(high)


def level_of(key, shape, split, least, high):
    loudness = 1.0
    for axis_at, shards_of in split:
        draws = jax.random.uniform(jax.random.fold_in(jax.random.fold_in(key, 6), axis_at), (shards_of,), jnp.float32, least / len(split), high / len(split))
        loudness = loudness * jnp.repeat(jnp.exp(draws), shape[axis_at] // shards_of).reshape((-1,) + (1,) * (len(shape) - 1 - axis_at))
    return loudness


def rank_table(number_of, skew):
    weights = [(1 << 20) // math.isqrt(rank ** skew) + 1 for rank in range(1, number_of + 1)]
    deviation = 1 + sum(weights) // (1 << 30)
    return np.cumsum(np.array([max(1, weight // deviation) for weight in weights]))


def ranked(key, extent, number_of, lean):
    grid = rank_table(number_of, lean)
    ticket = jax.random.randint(jax.random.fold_in(key, 1), extent, 0, int(grid[number_of - 1]))
    grade = jnp.searchsorted(jnp.asarray(grid, jnp.int32), ticket, side="right")
    return jax.random.permutation(jax.random.fold_in(key, 2), number_of)[grade].astype(jnp.int32)


def bell_draw(rng, extent, scale, bound, shards=(), kind=jnp.bfloat16):
    entries = jax.random.normal(rng, extent, jnp.float32) * scale
    if len(shards) > 0:
        entries = level_of(rng, extent, shards, -0.22, 0.18) * entries
    return jnp.clip(entries, min=-bound, max=bound).astype(kind)


def setup_inputs(seed: int = 0, part: int = 0) -> dict:
    streams_of = jax.random.split(jax.random.key(seed), 8)
    part_keys = jax.random.split(jax.random.fold_in(streams_of[7], part), 8)
    normed_layer_input = bell_draw(part_keys[0], (TOKENS, MODEL_WIDTH), 1.0, 6.0, ((0, 4), (1, 4)))
    key_value_gradient = bell_draw(part_keys[1], (TOKENS, 2 * KEY_VALUE_WIDTH), 1.0, 6.0, ((0, 4), (1, 4)))
    key_value_weight = bell_draw(streams_of[2], (MODEL_WIDTH, 2 * KEY_VALUE_WIDTH), MODEL_WIDTH ** -0.5, 0.0625, ((1, 4),))
    adapter_down_weight = bell_draw(streams_of[3], (ADAPTER_TOTAL, ADAPTER_RANK, MODEL_WIDTH), MODEL_WIDTH ** -0.5, 0.0625, ((0, 4), (2, 4)))
    adapter_up_weight = bell_draw(streams_of[4], (ADAPTER_TOTAL, ADAPTER_RANK, 2 * KEY_VALUE_WIDTH), ADAPTER_RANK ** -0.5, 1.5, ((0, 4), (2, 4)))
    segment_adapter = plant(ranked(part_keys[5], (SEGMENTS,), ADAPTER_TOTAL, 2), jax.random.fold_in(part_keys[5], 3), 0, ADAPTER_TOTAL - 1).astype(jnp.int32)
    slot_per_adapter = jax.random.permutation(streams_of[6], ADAPTER_TOTAL).astype(jnp.int32)
    return dict(normed_layer_input=normed_layer_input, key_value_gradient=key_value_gradient, key_value_weight=key_value_weight, adapter_down_weight=adapter_down_weight, adapter_up_weight=adapter_up_weight, segment_adapter=segment_adapter, slot_per_adapter=slot_per_adapter)


adapter_scale = 2.0


def reference(normed_layer_input, key_value_gradient, key_value_weight, adapter_down_weight, adapter_up_weight, segment_adapter, slot_per_adapter):
    chosen = slot_per_adapter[segment_adapter].astype(jnp.int32)
    input_blocks = normed_layer_input.reshape(SEGMENTS, SEG, MODEL_WIDTH)
    grad_blocks = key_value_gradient.reshape(SEGMENTS, SEG, 2 * KEY_VALUE_WIDTH)

    def per_segment(items):
        rows_in, rows_grad, adapter_slot = items
        down_projection = adapter_down_weight[adapter_slot]
        up_projection = adapter_up_weight[adapter_slot]
        low_rank_input = jnp.dot(rows_in, down_projection.T, preferred_element_type=jnp.float32)
        low_rank_gradient = jnp.dot(rows_grad, up_projection.T, preferred_element_type=jnp.float32)
        input_scaled = (adapter_scale * low_rank_input).astype(jnp.bfloat16)
        gradient_scaled = (adapter_scale * low_rank_gradient).astype(jnp.bfloat16)
        adapter_term = jnp.dot(gradient_scaled, down_projection, preferred_element_type=jnp.float32)
        term_down = jnp.dot(gradient_scaled.T, rows_in, preferred_element_type=jnp.float32)
        term_up = jnp.dot(input_scaled.T, rows_grad, preferred_element_type=jnp.float32)
        return adapter_term, term_down, term_up

    adapter_term, term_down, term_up = lax.map(per_segment, (input_blocks, grad_blocks, chosen))
    base_term = jnp.dot(key_value_gradient, key_value_weight.T, preferred_element_type=jnp.float32)
    grad_input = (base_term + adapter_term.reshape(TOKENS, MODEL_WIDTH)).astype(jnp.bfloat16)
    grad_down = jax.ops.segment_sum(term_down, chosen, ADAPTER_TOTAL)
    grad_up = jax.ops.segment_sum(term_up, chosen, ADAPTER_TOTAL)
    return grad_input, grad_down, grad_up
```

```python
import functools

import jax
import jax.numpy as jnp
from jax import lax
from jax.experimental import pallas as pl
from jax.experimental.pallas import tpu as pltpu
from jax.sharding import PartitionSpec as P

SEG = 128
MESH = pl.DeviceIdType.MESH
CHUNK = 256
FIRST = 4

adapter_scale = 2.0

NT = (((1,), (1,)), ((), ()))


def dot(a, b, dims=(((1,), (0,)), ((), ()))):
    return lax.dot_general(a, b, dims, preferred_element_type=jnp.float32)


def kernel(
    dp,
    rank,
    seg_ref,
    slot_ref,
    x_hbm,
    g_hbm,
    w_hbm,
    down_hbm,
    up_hbm,
    out_hbm,
    grad_down_hbm,
    grad_up_hbm,
    x,
    g,
    w_far,
    w_own,
    down,
    up,
    send,
    recv,
    acc,
    out,
    prod_in,
    prod_grad,
    low,
    low_mate,
    low_pair,
    low_peer,
    wide_grad,
    wide_in,
    rows_grad,
    dense_down,
    dense_up,
    send_down,
    send_up,
    recv_down,
    recv_up,
    final_down,
    final_up,
    load_sem,
    out_sem,
    g_send,
    g_recv,
    far_send,
    far_recv,
    own_send,
    own_recv,
    map_send,
    map_recv,
    low_send,
    low_recv,
    chunk_send,
    chunk_recv,
    term_send,
    term_recv,
):
    t = lax.axis_index("tensor")
    me = lax.axis_index("dp")
    mate = t + 1 - 2 * lax.rem(t, 2)
    peer = lax.rem(t + 2, 4)
    cross = 3 - t
    rows, feats = x.shape
    chunks = feats // CHUNK
    segs = rows // SEG
    held = down.shape[0] // dp
    slots = down.shape[0] // rank
    blocks = down.shape[0] // 128

    def local(src, dst, sem):
        return pltpu.make_async_copy(src, dst, sem)

    def remote(src, dst, send_sem, recv_sem, **where):
        return pltpu.make_async_remote_copy(
            src_ref=src, dst_ref=dst, send_sem=send_sem, recv_sem=recv_sem, device_id=where, device_id_type=MESH
        )

    def held_rows(ref, index):
        return ref.at[pl.ds(pl.multiple_of(index * held, held), held)]

    def chunk_rows(ref, base, k):
        return ref.at[pl.ds(pl.multiple_of(base * feats + k * CHUNK, CHUNK), CHUNK)]

    loads = [
        local(g_hbm, g.at[0], load_sem.at[0]),
        local(w_hbm.at[pl.ds(pl.multiple_of(peer * feats, feats), feats)], w_far.at[0], load_sem.at[1]),
        local(x_hbm, x, load_sem.at[2]),
        local(down_hbm, held_rows(down, me), load_sem.at[3]),
        local(up_hbm, held_rows(up, me), load_sem.at[4]),
        local(w_hbm.at[pl.ds(pl.multiple_of(t * feats, feats), feats)], w_own.at[0], load_sem.at[5]),
    ]
    for load in loads:
        load.start()

    barrier = pltpu.get_barrier_semaphore()
    pl.semaphore_signal(barrier, inc=1, device_id={"tensor": mate}, device_id_type=MESH)
    pl.semaphore_signal(barrier, inc=1, device_id={"tensor": peer}, device_id_type=MESH)
    for d in range(1, dp):
        pl.semaphore_signal(barrier, inc=1, device_id={"dp": lax.rem(me + d, dp)}, device_id_type=MESH)
    pl.semaphore_wait(barrier, dp + 1)

    copy_g = remote(g_hbm, g.at[1], g_send, g_recv, tensor=mate)
    copy_g.start()

    def copy_far(k):
        return remote(
            chunk_rows(w_hbm, cross, k), chunk_rows(w_far.at[1], 0, k), far_send.at[k], far_recv.at[k], tensor=mate
        )

    for k in range(chunks):
        copy_far(k).start()
    maps = []
    for d in range(1, dp):
        target = lax.rem(me + d, dp)
        maps.append(remote(up_hbm, held_rows(up, me), map_send.at[0, d], map_recv.at[0, d], dp=target))
        maps.append(remote(down_hbm, held_rows(down, me), map_send.at[1, d], map_recv.at[1, d], dp=target))
    for copy in maps:
        copy.start()
    copy_own = remote(
        w_hbm.at[pl.ds(pl.multiple_of(mate * feats, feats), feats)], w_own.at[1], own_send, own_recv, tensor=mate
    )
    copy_own.start()

    def copy_chunk(k):
        return remote(send.at[k], recv.at[k], chunk_send.at[k], chunk_recv.at[k], tensor=peer)

    def send_chunk(k, carry):
        copy_far(k).wait_recv()
        at = pl.ds(pl.multiple_of(k * CHUNK, CHUNK), CHUNK)
        part = dot(g[0], w_far[0, at, :], NT) + dot(g[1], w_far[1, at, :], NT)
        send[k] = part.astype(jnp.bfloat16)
        copy_chunk(k).start()
        return carry

    loads[0].wait()
    loads[1].wait()
    copy_g.wait_recv()
    lax.fori_loop(0, FIRST, send_chunk, 0)

    for load in loads[2:5]:
        load.wait()
    for copy in maps:
        copy.wait_recv()

    def project(b, carry):
        at = pl.ds(pl.multiple_of(b * 128, 128), 128)
        prod_in[at, :] = dot(down[at, :], x[...], NT)
        prod_grad[at, :] = dot(up[at, :], g[0], NT)
        return carry

    lax.fori_loop(0, blocks, project, 0)
    chosen = []
    for s in range(segs):
        adapter = jnp.full((rank, SEG), seg_ref[s], jnp.int32)
        slot = jnp.zeros((rank, SEG), jnp.int32)
        for j in range(slots):
            slot = jnp.where(adapter == j, jnp.full((rank, SEG), slot_ref[j], jnp.int32), slot)
        chosen.append(slot)
    low[...] = jnp.zeros_like(low)

    def select(a, carry):
        at = pl.ds(pl.multiple_of(a * rank, rank), rank)
        for s in range(segs):
            span = slice(s * SEG, (s + 1) * SEG)
            low[0:rank, span] = jnp.where(chosen[s] == a, prod_in[at, span], low[0:rank, span])
            low[rank : 2 * rank, span] = jnp.where(chosen[s] == a, prod_grad[at, span], low[rank : 2 * rank, span])
        return carry

    lax.fori_loop(0, slots, select, 0)
    copy_low = remote(low, low_mate, low_send.at[0], low_recv.at[0], tensor=mate)
    copy_low.start()
    copy_low.wait_recv()
    low_pair[...] = low[...] + low_mate[...]
    copy_pair = remote(low_pair, low_peer, low_send.at[1], low_recv.at[1], tensor=peer)
    copy_pair.start()

    lax.fori_loop(FIRST, chunks, send_chunk, 0)

    loads[5].wait()
    copy_own.wait_recv()

    def own_chunk(k, carry):
        at = pl.ds(pl.multiple_of(k * CHUNK, CHUNK), CHUNK)
        acc[k] = dot(g[0], w_own[0, at, :], NT) + dot(g[1], w_own[1, at, :], NT)
        return carry

    lax.fori_loop(0, chunks, own_chunk, 0)

    copy_pair.wait_recv()
    scaled = (adapter_scale * (low_pair[...] + low_peer[...])).astype(jnp.bfloat16).astype(jnp.float32)

    def widen(a, carry):
        at = pl.ds(pl.multiple_of(a * rank, rank), rank)
        for s in range(segs):
            span = slice(s * SEG, (s + 1) * SEG)
            wide_in[at, span] = jnp.where(chosen[s] == a, scaled[0:rank, span], 0.0)
            wide_grad[at, span] = jnp.where(chosen[s] == a, scaled[rank : 2 * rank, span], 0.0)
        return carry

    lax.fori_loop(0, slots, widen, 0)

    def terms(b, carry):
        at = pl.ds(pl.multiple_of(b * 128, 128), 128)
        left = wide_grad[at, :].astype(jnp.bfloat16)
        for n in range(feats // 512):
            span = slice(n * 512, (n + 1) * 512)
            value = dot(left, x[:, span])
            dense_down[at, span] = value
            send_down[at, span] = value.astype(jnp.bfloat16)
        value = dot(wide_in[at, :].astype(jnp.bfloat16), g[0])
        dense_up[at, :] = value
        send_up[at, :] = value.astype(jnp.bfloat16)
        return carry

    lax.fori_loop(0, blocks, terms, 0)
    copies = []
    for d in range(1, dp):
        target = lax.rem(me + d, dp)
        copies.append(
            remote(held_rows(send_down, target), recv_down.at[d], term_send.at[0, d], term_recv.at[0, d], dp=target)
        )
        copies.append(
            remote(held_rows(send_up, target), recv_up.at[d], term_send.at[1, d], term_recv.at[1, d], dp=target)
        )
    for copy in copies:
        copy.start()

    for b in range(blocks):
        span = slice(b * 128, (b + 1) * 128)
        rows_grad[:, span] = wide_grad[span, :].T.astype(jnp.bfloat16)

    for k in range(chunks):
        acc[k] = acc[k] + dot(rows_grad[...], down[:, k * CHUNK : (k + 1) * CHUNK])

    outs = []
    for k in range(chunks):
        copy_chunk(k).wait_recv()
        out[k] = (acc[k] + recv[k].astype(jnp.float32)).astype(jnp.bfloat16)
        outs.append(local(out.at[k], out_hbm.at[:, pl.ds(k * CHUNK, CHUNK)], out_sem.at[k]))
        outs[k].start()

    for copy in copies:
        copy.wait_recv()
    mine = pl.ds(pl.multiple_of(me * held, held), held)
    final_down[...] = dense_down[mine, :]
    final_up[...] = dense_up[mine, :]
    for d in range(1, dp):
        final_down[...] += recv_down[d].astype(jnp.float32)
        final_up[...] += recv_up[d].astype(jnp.float32)
    outs.append(local(final_down, grad_down_hbm, out_sem.at[chunks]))
    outs.append(local(final_up, grad_up_hbm, out_sem.at[chunks + 1]))
    outs[chunks].start()
    outs[chunks + 1].start()

    copy_g.wait_send()
    copy_own.wait_send()
    copy_low.wait_send()
    copy_pair.wait_send()
    for k in range(chunks):
        copy_far(k).wait_send()
        copy_chunk(k).wait_send()
    for copy in maps + copies:
        copy.wait_send()
    for copy in outs:
        copy.wait()


def shards(
    dp,
    normed_layer_input,
    key_value_gradient,
    key_value_weight,
    adapter_down_weight,
    adapter_up_weight,
    segment_adapter,
    slot_per_adapter,
):
    rows, feats = normed_layer_input.shape
    cols = key_value_gradient.shape[1]
    count, rank, _ = adapter_down_weight.shape
    held = count * rank
    wide = dp * held
    chunks = feats // CHUNK
    bf16, f32 = jnp.bfloat16, jnp.float32
    vmem, dma = pltpu.VMEM, pltpu.SemaphoreType.DMA
    anywhere = pl.BlockSpec(memory_space=pl.ANY)
    smem = pl.BlockSpec(memory_space=pltpu.SMEM)
    grad_input, grad_down, grad_up = pl.pallas_call(
        functools.partial(kernel, dp, rank),
        out_shape=(
            jax.ShapeDtypeStruct((rows, feats), bf16),
            jax.ShapeDtypeStruct((held, feats), f32),
            jax.ShapeDtypeStruct((held, cols), f32),
        ),
        in_specs=[smem, smem] + [anywhere] * 5,
        out_specs=(anywhere,) * 3,
        scratch_shapes=[
            vmem((rows, feats), bf16),
            vmem((2, rows, cols), bf16),
            vmem((2, feats, cols), bf16),
            vmem((2, feats, cols), bf16),
            vmem((wide, feats), bf16),
            vmem((wide, cols), bf16),
            vmem((chunks, rows, CHUNK), bf16),
            vmem((chunks, rows, CHUNK), bf16),
            vmem((chunks, rows, CHUNK), f32),
            vmem((chunks, rows, CHUNK), bf16),
            vmem((wide, rows), f32),
            vmem((wide, rows), f32),
            vmem((2 * rank, rows), f32),
            vmem((2 * rank, rows), f32),
            vmem((2 * rank, rows), f32),
            vmem((2 * rank, rows), f32),
            vmem((wide, rows), f32),
            vmem((wide, rows), f32),
            vmem((rows, wide), bf16),
            vmem((wide, feats), f32),
            vmem((wide, cols), f32),
            vmem((wide, feats), bf16),
            vmem((wide, cols), bf16),
            vmem((dp, held, feats), bf16),
            vmem((dp, held, cols), bf16),
            vmem((held, feats), f32),
            vmem((held, cols), f32),
            dma((6,)),
            dma((chunks + 2,)),
            dma,
            dma,
            dma((chunks,)),
            dma((chunks,)),
            dma,
            dma,
            dma((2, dp)),
            dma((2, dp)),
            dma((2,)),
            dma((2,)),
            dma((chunks,)),
            dma((chunks,)),
            dma((2, dp)),
            dma((2, dp)),
        ],
        compiler_params=pltpu.CompilerParams(
            collective_id=0, has_side_effects=True, vmem_limit_bytes=60 * 1024 * 1024
        ),
    )(
        segment_adapter,
        slot_per_adapter,
        normed_layer_input,
        key_value_gradient,
        key_value_weight,
        adapter_down_weight.reshape(held, feats),
        adapter_up_weight.reshape(held, cols),
    )
    return grad_input, grad_down.reshape(count, rank, feats), grad_up.reshape(count, rank, cols)


def solution(mesh):
    placed = (
        P(("groups", "dp"), "tensor"),
        P(("groups", "dp"), "tensor"),
        P(None, "tensor"),
        P("dp", None, "tensor"),
        P("dp", None, "tensor"),
        P(("groups", "dp")),
        P(),
    )
    return jax.shard_map(
        functools.partial(shards, mesh.shape["dp"]),
        mesh=mesh,
        in_specs=placed,
        out_specs=(
            P(("groups", "dp"), "tensor"),
            P(("groups", "dp"), None, "tensor"),
            P(("groups", "dp"), None, "tensor"),
        ),
        check_vma=False,
    )
```

```python
import functools

import jax
import jax.numpy as jnp
from jax import lax
from jax.experimental import pallas as pl
from jax.experimental.pallas import tpu as pltpu
from jax.sharding import PartitionSpec as P

SEG = 128
MESH = pl.DeviceIdType.MESH
CHUNK = 256
FIRST = 4

adapter_scale = 2.0

NT = (((1,), (1,)), ((), ()))


def dot(a, b, dims=(((1,), (0,)), ((), ()))):
    return lax.dot_general(a, b, dims, preferred_element_type=jnp.float32)


def kernel(
    dp,
    rank,
    seg_ref,
    slot_ref,
    x_hbm,
    g_hbm,
    w_hbm,
    down_hbm,
    up_hbm,
    out,
    final_down,
    final_up,
    x,
    g,
    w_far,
    w_own,
    down,
    up,
    send,
    recv,
    acc,
    prod_in,
    prod_grad,
    low,
    low_mate,
    low_pair,
    low_peer,
    wide_grad,
    wide_in,
    rows_grad,
    dense_down,
    dense_up,
    send_down,
    send_up,
    recv_down,
    recv_up,
    load_sem,
    g_send,
    g_recv,
    far_send,
    far_recv,
    own_send,
    own_recv,
    map_send,
    map_recv,
    low_send,
    low_recv,
    chunk_send,
    chunk_recv,
    term_send,
    term_recv,
):
    t = lax.axis_index("tensor")
    me = lax.axis_index("dp")
    mate = t + 1 - 2 * lax.rem(t, 2)
    peer = lax.rem(t + 2, 4)
    cross = 3 - t
    rows, feats = x.shape
    chunks = feats // CHUNK
    segs = rows // SEG
    held = down.shape[0] // dp
    slots = down.shape[0] // rank
    blocks = down.shape[0] // 128

    def local(src, dst, sem):
        return pltpu.make_async_copy(src, dst, sem)

    def remote(src, dst, send_sem, recv_sem, **where):
        return pltpu.make_async_remote_copy(
            src_ref=src, dst_ref=dst, send_sem=send_sem, recv_sem=recv_sem, device_id=where, device_id_type=MESH
        )

    def held_rows(ref, index):
        return ref.at[pl.ds(pl.multiple_of(index * held, held), held)]

    def chunk_rows(ref, base, k):
        return ref.at[pl.ds(pl.multiple_of(base * feats + k * CHUNK, CHUNK), CHUNK)]

    loads = [
        local(g_hbm, g.at[0], load_sem.at[0]),
        local(w_hbm.at[pl.ds(pl.multiple_of(peer * feats, feats), feats)], w_far.at[0], load_sem.at[1]),
        local(x_hbm, x, load_sem.at[2]),
        local(down_hbm, held_rows(down, me), load_sem.at[3]),
        local(up_hbm, held_rows(up, me), load_sem.at[4]),
        local(w_hbm.at[pl.ds(pl.multiple_of(t * feats, feats), feats)], w_own.at[0], load_sem.at[5]),
    ]
    for load in loads:
        load.start()

    barrier = pltpu.get_barrier_semaphore()
    pl.semaphore_signal(barrier, inc=1, device_id={"tensor": mate}, device_id_type=MESH)
    pl.semaphore_signal(barrier, inc=1, device_id={"tensor": peer}, device_id_type=MESH)
    for d in range(1, dp):
        pl.semaphore_signal(barrier, inc=1, device_id={"dp": lax.rem(me + d, dp)}, device_id_type=MESH)
    pl.semaphore_wait(barrier, dp + 1)

    copy_g = remote(g_hbm, g.at[1], g_send, g_recv, tensor=mate)
    copy_g.start()

    def copy_far(k):
        return remote(
            chunk_rows(w_hbm, cross, k), chunk_rows(w_far.at[1], 0, k), far_send.at[k], far_recv.at[k], tensor=mate
        )

    for k in range(chunks):
        copy_far(k).start()
    maps = []
    for d in range(1, dp):
        target = lax.rem(me + d, dp)
        maps.append(remote(up_hbm, held_rows(up, me), map_send.at[0, d], map_recv.at[0, d], dp=target))
        maps.append(remote(down_hbm, held_rows(down, me), map_send.at[1, d], map_recv.at[1, d], dp=target))
    for copy in maps:
        copy.start()
    copy_own = remote(
        w_hbm.at[pl.ds(pl.multiple_of(mate * feats, feats), feats)], w_own.at[1], own_send, own_recv, tensor=mate
    )
    copy_own.start()

    def copy_chunk(k):
        return remote(send.at[k], recv.at[k], chunk_send.at[k], chunk_recv.at[k], tensor=peer)

    def send_chunk(k, carry):
        copy_far(k).wait_recv()
        at = pl.ds(pl.multiple_of(k * CHUNK, CHUNK), CHUNK)
        part = dot(g[0], w_far[0, at, :], NT) + dot(g[1], w_far[1, at, :], NT)
        send[k] = part.astype(jnp.bfloat16)
        copy_chunk(k).start()
        return carry

    loads[0].wait()
    loads[1].wait()
    copy_g.wait_recv()
    lax.fori_loop(0, FIRST, send_chunk, 0)

    for load in loads[2:5]:
        load.wait()
    for copy in maps:
        copy.wait_recv()

    def project(b, carry):
        at = pl.ds(pl.multiple_of(b * 128, 128), 128)
        prod_in[at, :] = dot(down[at, :], x[...], NT)
        prod_grad[at, :] = dot(up[at, :], g[0], NT)
        return carry

    lax.fori_loop(0, blocks, project, 0)
    chosen = []
    for s in range(segs):
        adapter = jnp.full((rank, SEG), seg_ref[s], jnp.int32)
        slot = jnp.zeros((rank, SEG), jnp.int32)
        for j in range(slots):
            slot = jnp.where(adapter == j, jnp.full((rank, SEG), slot_ref[j], jnp.int32), slot)
        chosen.append(slot)
    low[...] = jnp.zeros_like(low)

    def select(a, carry):
        at = pl.ds(pl.multiple_of(a * rank, rank), rank)
        for s in range(segs):
            span = slice(s * SEG, (s + 1) * SEG)
            low[0:rank, span] = jnp.where(chosen[s] == a, prod_in[at, span], low[0:rank, span])
            low[rank : 2 * rank, span] = jnp.where(chosen[s] == a, prod_grad[at, span], low[rank : 2 * rank, span])
        return carry

    lax.fori_loop(0, slots, select, 0)
    copy_low = remote(low, low_mate, low_send.at[0], low_recv.at[0], tensor=mate)
    copy_low.start()
    copy_low.wait_recv()
    low_pair[...] = low[...] + low_mate[...]
    half = pl.ds(pl.multiple_of(lax.rem(t, 2) * rank, rank), rank)
    copy_pair = remote(low_pair.at[half], low_peer.at[half], low_send.at[1], low_recv.at[1], tensor=peer)
    copy_pair.start()

    lax.fori_loop(FIRST, chunks, send_chunk, 0)

    loads[5].wait()
    copy_own.wait_recv()

    def own_chunk(k, carry):
        at = pl.ds(pl.multiple_of(k * CHUNK, CHUNK), CHUNK)
        acc[k] = dot(g[0], w_own[0, at, :], NT) + dot(g[1], w_own[1, at, :], NT)
        return carry

    lax.fori_loop(0, chunks, own_chunk, 0)

    copy_pair.wait_recv()
    copy_half = remote(low_peer.at[half], low_peer.at[half], low_send.at[2], low_recv.at[2], tensor=mate)
    copy_half.start()
    copy_half.wait_recv()
    scaled = (adapter_scale * (low_pair[...] + low_peer[...])).astype(jnp.bfloat16).astype(jnp.float32)

    def widen(a, carry):
        at = pl.ds(pl.multiple_of(a * rank, rank), rank)
        for s in range(segs):
            span = slice(s * SEG, (s + 1) * SEG)
            wide_in[at, span] = jnp.where(chosen[s] == a, scaled[0:rank, span], 0.0)
            wide_grad[at, span] = jnp.where(chosen[s] == a, scaled[rank : 2 * rank, span], 0.0)
        return carry

    lax.fori_loop(0, slots, widen, 0)

    def terms(b, carry):
        at = pl.ds(pl.multiple_of(b * 128, 128), 128)
        left = wide_grad[at, :].astype(jnp.bfloat16)
        for n in range(feats // 512):
            span = slice(n * 512, (n + 1) * 512)
            value = dot(left, x[:, span])
            dense_down[at, span] = value
            send_down[at, span] = value.astype(jnp.bfloat16)
        value = dot(wide_in[at, :].astype(jnp.bfloat16), g[0])
        dense_up[at, :] = value
        send_up[at, :] = value.astype(jnp.bfloat16)
        return carry

    lax.fori_loop(0, blocks, terms, 0)
    copies = []
    for d in range(1, dp):
        target = lax.rem(me + d, dp)
        copies.append(
            remote(held_rows(send_down, target), recv_down.at[d], term_send.at[0, d], term_recv.at[0, d], dp=target)
        )
        copies.append(
            remote(held_rows(send_up, target), recv_up.at[d], term_send.at[1, d], term_recv.at[1, d], dp=target)
        )
    for copy in copies:
        copy.start()

    for b in range(blocks):
        span = slice(b * 128, (b + 1) * 128)
        rows_grad[:, span] = wide_grad[span, :].T.astype(jnp.bfloat16)

    for k in range(chunks):
        acc[k] = acc[k] + dot(rows_grad[...], down[:, k * CHUNK : (k + 1) * CHUNK])

    def finish(k):
        copy_chunk(k).wait_recv()
        out[:, k * CHUNK : (k + 1) * CHUNK] = (acc[k] + recv[k].astype(jnp.float32)).astype(jnp.bfloat16)

    for k in range(chunks - 1):
        finish(k)

    for copy in copies:
        copy.wait_recv()
    mine = pl.ds(pl.multiple_of(me * held, held), held)
    final_down[...] = dense_down[mine, :]
    final_up[...] = dense_up[mine, :]
    for d in range(1, dp):
        final_down[...] += recv_down[d].astype(jnp.float32)
        final_up[...] += recv_up[d].astype(jnp.float32)

    copy_g.wait_send()
    copy_own.wait_send()
    copy_low.wait_send()
    copy_pair.wait_send()
    copy_half.wait_send()
    for k in range(chunks):
        copy_far(k).wait_send()
    for k in range(chunks):
        copy_chunk(k).wait_send()
    for copy in maps + copies:
        copy.wait_send()
    finish(chunks - 1)


def write(out, grad_down, grad_up, out_hbm, grad_down_hbm, grad_up_hbm, sem):
    copies = [
        pltpu.make_async_copy(out, out_hbm, sem.at[0]),
        pltpu.make_async_copy(grad_down, grad_down_hbm, sem.at[1]),
        pltpu.make_async_copy(grad_up, grad_up_hbm, sem.at[2]),
    ]
    for copy in copies:
        copy.start()
    for copy in copies:
        copy.wait()


def shards(
    dp,
    normed_layer_input,
    key_value_gradient,
    key_value_weight,
    adapter_down_weight,
    adapter_up_weight,
    segment_adapter,
    slot_per_adapter,
):
    rows, feats = normed_layer_input.shape
    cols = key_value_gradient.shape[1]
    count, rank, _ = adapter_down_weight.shape
    held = count * rank
    wide = dp * held
    chunks = feats // CHUNK
    bf16, f32 = jnp.bfloat16, jnp.float32
    vmem, dma = pltpu.VMEM, pltpu.SemaphoreType.DMA
    anywhere = pl.BlockSpec(memory_space=pl.ANY)
    smem = pl.BlockSpec(memory_space=pltpu.SMEM)
    inside = pl.BlockSpec(memory_space=pltpu.VMEM)
    made = pl.pallas_call(
        functools.partial(kernel, dp, rank),
        out_shape=(vmem((rows, feats), bf16), vmem((held, feats), f32), vmem((held, cols), f32)),
        in_specs=[smem, smem] + [anywhere] * 5,
        out_specs=(inside,) * 3,
        scratch_shapes=[
            vmem((rows, feats), bf16),
            vmem((2, rows, cols), bf16),
            vmem((2, feats, cols), bf16),
            vmem((2, feats, cols), bf16),
            vmem((wide, feats), bf16),
            vmem((wide, cols), bf16),
            vmem((chunks, rows, CHUNK), bf16),
            vmem((chunks, rows, CHUNK), bf16),
            vmem((chunks, rows, CHUNK), f32),
            vmem((wide, rows), f32),
            vmem((wide, rows), f32),
            vmem((2 * rank, rows), f32),
            vmem((2 * rank, rows), f32),
            vmem((2 * rank, rows), f32),
            vmem((2 * rank, rows), f32),
            vmem((wide, rows), f32),
            vmem((wide, rows), f32),
            vmem((rows, wide), bf16),
            vmem((wide, feats), f32),
            vmem((wide, cols), f32),
            vmem((wide, feats), bf16),
            vmem((wide, cols), bf16),
            vmem((dp, held, feats), bf16),
            vmem((dp, held, cols), bf16),
            dma((6,)),
            dma,
            dma,
            dma((chunks,)),
            dma((chunks,)),
            dma,
            dma,
            dma((2, dp)),
            dma((2, dp)),
            dma((3,)),
            dma((3,)),
            dma((chunks,)),
            dma((chunks,)),
            dma((2, dp)),
            dma((2, dp)),
        ],
        compiler_params=pltpu.CompilerParams(
            collective_id=0, has_side_effects=True, vmem_limit_bytes=60 * 1024 * 1024
        ),
    )(
        segment_adapter,
        slot_per_adapter,
        normed_layer_input,
        key_value_gradient,
        key_value_weight,
        adapter_down_weight.reshape(held, feats),
        adapter_up_weight.reshape(held, cols),
    )
    grad_input, grad_down, grad_up = pl.pallas_call(
        write,
        out_shape=(
            jax.ShapeDtypeStruct((rows, feats), bf16),
            jax.ShapeDtypeStruct((held, feats), f32),
            jax.ShapeDtypeStruct((held, cols), f32),
        ),
        in_specs=[inside] * 3,
        out_specs=(anywhere,) * 3,
        scratch_shapes=[dma((3,))],
    )(*made)
    return grad_input, grad_down.reshape(count, rank, feats), grad_up.reshape(count, rank, cols)


def solution(mesh):
    placed = (
        P(("groups", "dp"), "tensor"),
        P(("groups", "dp"), "tensor"),
        P(None, "tensor"),
        P("dp", None, "tensor"),
        P("dp", None, "tensor"),
        P(("groups", "dp")),
        P(),
    )
    return jax.shard_map(
        functools.partial(shards, mesh.shape["dp"]),
        mesh=mesh,
        in_specs=placed,
        out_specs=(
            P(("groups", "dp"), "tensor"),
            P(("groups", "dp"), None, "tensor"),
            P(("groups", "dp"), None, "tensor"),
        ),
        check_vma=False,
    )
```

```python
import functools
import math

import jax
import jax.numpy as jnp
from jax import lax
from jax.experimental import pallas as pl
from jax.experimental.pallas import tpu as pltpu
from jax.sharding import PartitionSpec as P

SEG = 128
MESH = pl.DeviceIdType.MESH
CHUNK = 256
FIRST = 4

adapter_scale = 2.0

NT = (((1,), (1,)), ((), ()))


def dot(a, b, dims=(((1,), (0,)), ((), ()))):
    return lax.dot_general(a, b, dims, preferred_element_type=jnp.float32)


def kernel(
    dp,
    rank,
    seg_hbm,
    slot_hbm,
    x_hbm,
    g_hbm,
    w_hbm,
    down_hbm,
    up_hbm,
    out,
    final_down,
    final_up,
    x,
    g,
    w_far,
    w_own,
    down,
    up,
    send,
    recv,
    acc,
    prod_in,
    prod_grad,
    low,
    low_mate,
    low_pair,
    low_peer,
    wide_grad,
    wide_in,
    rows_grad,
    dense_down,
    dense_up,
    send_down,
    send_up,
    recv_down,
    recv_up,
    seg_ref,
    slot_ref,
    load_sem,
    g_send,
    g_recv,
    far_send,
    far_recv,
    own_send,
    own_recv,
    map_send,
    map_recv,
    low_send,
    low_recv,
    chunk_send,
    chunk_recv,
    term_send,
    term_recv,
):
    t = lax.axis_index("tensor")
    me = lax.axis_index("dp")
    mate = t + 1 - 2 * lax.rem(t, 2)
    peer = lax.rem(t + 2, 4)
    cross = 3 - t
    rows, feats = x.shape
    chunks = feats // CHUNK
    segs = rows // SEG
    held = down.shape[0] // dp
    slots = down.shape[0] // rank
    blocks = down.shape[0] // 128

    def local(src, dst, sem):
        return pltpu.make_async_copy(src, dst, sem)

    def remote(src, dst, send_sem, recv_sem, **where):
        return pltpu.make_async_remote_copy(
            src_ref=src, dst_ref=dst, send_sem=send_sem, recv_sem=recv_sem, device_id=where, device_id_type=MESH
        )

    def held_rows(ref, index):
        return ref.at[pl.ds(pl.multiple_of(index * held, held), held)]

    def chunk_rows(ref, base, k):
        return ref.at[pl.ds(pl.multiple_of(base * feats + k * CHUNK, CHUNK), CHUNK)]

    loads = [
        local(g_hbm, g.at[0], load_sem.at[0]),
        local(w_hbm.at[pl.ds(pl.multiple_of(peer * feats, feats), feats)], w_far.at[0], load_sem.at[1]),
        local(x_hbm, x, load_sem.at[2]),
        local(down_hbm, held_rows(down, me), load_sem.at[3]),
        local(up_hbm, held_rows(up, me), load_sem.at[4]),
        local(w_hbm.at[pl.ds(pl.multiple_of(t * feats, feats), feats)], w_own.at[0], load_sem.at[5]),
        local(seg_hbm, seg_ref, load_sem.at[6]),
        local(slot_hbm, slot_ref, load_sem.at[7]),
    ]
    for load in loads:
        load.start()

    barrier = pltpu.get_barrier_semaphore()
    pl.semaphore_signal(barrier, inc=1, device_id={"tensor": mate}, device_id_type=MESH)
    pl.semaphore_signal(barrier, inc=1, device_id={"tensor": peer}, device_id_type=MESH)
    for d in range(1, dp):
        pl.semaphore_signal(barrier, inc=1, device_id={"dp": lax.rem(me + d, dp)}, device_id_type=MESH)
    pl.semaphore_wait(barrier, dp + 1)

    copy_g = remote(g_hbm, g.at[1], g_send, g_recv, tensor=mate)
    copy_g.start()

    def copy_far(k):
        return remote(
            chunk_rows(w_hbm, cross, k), chunk_rows(w_far.at[1], 0, k), far_send.at[k], far_recv.at[k], tensor=mate
        )

    for k in range(chunks):
        copy_far(k).start()
    maps = []
    for d in range(1, dp):
        target = lax.rem(me + d, dp)
        maps.append(remote(up_hbm, held_rows(up, me), map_send.at[0, d], map_recv.at[0, d], dp=target))
        maps.append(remote(down_hbm, held_rows(down, me), map_send.at[1, d], map_recv.at[1, d], dp=target))
    for copy in maps:
        copy.start()
    copy_own = remote(
        w_hbm.at[pl.ds(pl.multiple_of(mate * feats, feats), feats)], w_own.at[1], own_send, own_recv, tensor=mate
    )
    copy_own.start()

    def copy_chunk(k):
        return remote(send.at[k], recv.at[k], chunk_send.at[k], chunk_recv.at[k], tensor=peer)

    def send_chunk(k, carry):
        copy_far(k).wait_recv()
        at = pl.ds(pl.multiple_of(k * CHUNK, CHUNK), CHUNK)
        part = dot(g[0], w_far[0, at, :], NT) + dot(g[1], w_far[1, at, :], NT)
        send[k] = part.astype(jnp.bfloat16)
        copy_chunk(k).start()
        return carry

    loads[0].wait()
    loads[1].wait()
    copy_g.wait_recv()
    lax.fori_loop(0, FIRST, send_chunk, 0)

    for load in loads[2:5] + loads[6:8]:
        load.wait()
    for copy in maps:
        copy.wait_recv()

    def project(b, carry):
        at = pl.ds(pl.multiple_of(b * 128, 128), 128)
        prod_in[at, :] = dot(down[at, :], x[...], NT)
        prod_grad[at, :] = dot(up[at, :], g[0], NT)
        return carry

    lax.fori_loop(0, blocks, project, 0)
    chosen = []
    for s in range(segs):
        adapter = jnp.full((rank, SEG), seg_ref[s], jnp.int32)
        slot = jnp.zeros((rank, SEG), jnp.int32)
        for j in range(slots):
            slot = jnp.where(adapter == j, jnp.full((rank, SEG), slot_ref[j], jnp.int32), slot)
        chosen.append(slot)
    low[...] = jnp.zeros_like(low)

    def select(a, carry):
        at = pl.ds(pl.multiple_of(a * rank, rank), rank)
        for s in range(segs):
            span = slice(s * SEG, (s + 1) * SEG)
            low[0:rank, span] = jnp.where(chosen[s] == a, prod_in[at, span], low[0:rank, span])
            low[rank : 2 * rank, span] = jnp.where(chosen[s] == a, prod_grad[at, span], low[rank : 2 * rank, span])
        return carry

    lax.fori_loop(0, slots, select, 0)
    copy_low = remote(low, low_mate, low_send.at[0], low_recv.at[0], tensor=mate)
    copy_low.start()
    copy_low.wait_recv()
    low_pair[...] = low[...] + low_mate[...]
    half = pl.ds(pl.multiple_of(lax.rem(t, 2) * rank, rank), rank)
    copy_pair = remote(low_pair.at[half], low_peer.at[half], low_send.at[1], low_recv.at[1], tensor=peer)
    copy_pair.start()

    lax.fori_loop(FIRST, chunks, send_chunk, 0)

    loads[5].wait()
    copy_own.wait_recv()

    def own_chunk(k, carry):
        at = pl.ds(pl.multiple_of(k * CHUNK, CHUNK), CHUNK)
        acc[k] = dot(g[0], w_own[0, at, :], NT) + dot(g[1], w_own[1, at, :], NT)
        return carry

    lax.fori_loop(0, chunks, own_chunk, 0)

    copy_pair.wait_recv()
    copy_half = remote(low_peer.at[half], low_peer.at[half], low_send.at[2], low_recv.at[2], tensor=mate)
    copy_half.start()
    copy_half.wait_recv()
    scaled = (adapter_scale * (low_pair[...] + low_peer[...])).astype(jnp.bfloat16).astype(jnp.float32)

    def widen(a, carry):
        at = pl.ds(pl.multiple_of(a * rank, rank), rank)
        for s in range(segs):
            span = slice(s * SEG, (s + 1) * SEG)
            wide_in[at, span] = jnp.where(chosen[s] == a, scaled[0:rank, span], 0.0)
            wide_grad[at, span] = jnp.where(chosen[s] == a, scaled[rank : 2 * rank, span], 0.0)
        return carry

    lax.fori_loop(0, slots, widen, 0)

    def terms(b, carry):
        at = pl.ds(pl.multiple_of(b * 128, 128), 128)
        left = wide_grad[at, :].astype(jnp.bfloat16)
        for n in range(feats // 512):
            span = slice(n * 512, (n + 1) * 512)
            value = dot(left, x[:, span])
            dense_down[at, span] = value
            send_down[at, span] = value.astype(jnp.bfloat16)
        value = dot(wide_in[at, :].astype(jnp.bfloat16), g[0])
        dense_up[at, :] = value
        send_up[at, :] = value.astype(jnp.bfloat16)
        return carry

    lax.fori_loop(0, blocks, terms, 0)
    copies = []
    for d in range(1, dp):
        target = lax.rem(me + d, dp)
        copies.append(
            remote(held_rows(send_down, target), recv_down.at[d], term_send.at[0, d], term_recv.at[0, d], dp=target)
        )
        copies.append(
            remote(held_rows(send_up, target), recv_up.at[d], term_send.at[1, d], term_recv.at[1, d], dp=target)
        )
    for copy in copies:
        copy.start()

    for b in range(blocks):
        span = slice(b * 128, (b + 1) * 128)
        rows_grad[:, span] = wide_grad[span, :].T.astype(jnp.bfloat16)

    for k in range(chunks):
        acc[k] = acc[k] + dot(rows_grad[...], down[:, k * CHUNK : (k + 1) * CHUNK])

    def finish(k):
        copy_chunk(k).wait_recv()
        out[:, k * CHUNK : (k + 1) * CHUNK] = (acc[k] + recv[k].astype(jnp.float32)).astype(jnp.bfloat16)

    for k in range(chunks - 1):
        finish(k)

    for copy in copies:
        copy.wait_recv()
    mine = pl.ds(pl.multiple_of(me * held, held), held)
    final_down[...] = dense_down[mine, :]
    final_up[...] = dense_up[mine, :]
    for d in range(1, dp):
        final_down[...] += recv_down[d].astype(jnp.float32)
        final_up[...] += recv_up[d].astype(jnp.float32)

    copy_g.wait_send()
    copy_own.wait_send()
    copy_low.wait_send()
    copy_pair.wait_send()
    copy_half.wait_send()
    for k in range(chunks):
        copy_far(k).wait_send()
    for k in range(chunks):
        copy_chunk(k).wait_send()
    for copy in maps + copies:
        copy.wait_send()
    finish(chunks - 1)


def write(out, grad_down, grad_up, out_hbm, grad_down_hbm, grad_up_hbm, sem):
    copies = [
        pltpu.make_async_copy(out, out_hbm, sem.at[0]),
        pltpu.make_async_copy(grad_down, grad_down_hbm, sem.at[1]),
        pltpu.make_async_copy(grad_up, grad_up_hbm, sem.at[2]),
    ]
    for copy in copies:
        copy.start()
    for copy in copies:
        copy.wait()


def shards(
    dp,
    normed_layer_input,
    key_value_gradient,
    key_value_weight,
    adapter_down_weight,
    adapter_up_weight,
    segment_adapter,
    slot_per_adapter,
):
    rows, feats = normed_layer_input.shape
    cols = key_value_gradient.shape[1]
    count, rank, _ = adapter_down_weight.shape
    held = count * rank
    wide = dp * held
    chunks = feats // CHUNK
    bf16, f32 = jnp.bfloat16, jnp.float32
    vmem, dma = pltpu.VMEM, pltpu.SemaphoreType.DMA
    anywhere = pl.BlockSpec(memory_space=pl.ANY)
    buffers = [
        vmem((rows, feats), bf16),
        vmem((2, rows, cols), bf16),
        vmem((2, feats, cols), bf16),
        vmem((2, feats, cols), bf16),
        vmem((wide, feats), bf16),
        vmem((wide, cols), bf16),
        vmem((chunks, rows, CHUNK), bf16),
        vmem((chunks, rows, CHUNK), bf16),
        vmem((chunks, rows, CHUNK), f32),
        vmem((wide, rows), f32),
        vmem((wide, rows), f32),
        vmem((2 * rank, rows), f32),
        vmem((2 * rank, rows), f32),
        vmem((2 * rank, rows), f32),
        vmem((2 * rank, rows), f32),
        vmem((wide, rows), f32),
        vmem((wide, rows), f32),
        vmem((rows, wide), bf16),
        vmem((wide, feats), f32),
        vmem((wide, cols), f32),
        vmem((wide, feats), bf16),
        vmem((wide, cols), bf16),
        vmem((dp, held, feats), bf16),
        vmem((dp, held, cols), bf16),
    ]
    used = sum(math.prod(buffer.shape) * jnp.dtype(buffer.dtype).itemsize for buffer in buffers)
    inside = pl.BlockSpec(memory_space=pltpu.VMEM)
    made = pl.pallas_call(
        functools.partial(kernel, dp, rank),
        out_shape=(vmem((rows, feats), bf16), vmem((held, feats), f32), vmem((held, cols), f32)),
        in_specs=[anywhere] * 7,
        out_specs=(inside,) * 3,
        scratch_shapes=buffers
        + [
            pltpu.SMEM(segment_adapter.shape, jnp.int32),
            pltpu.SMEM(slot_per_adapter.shape, jnp.int32),
            dma((8,)),
            dma,
            dma,
            dma((chunks,)),
            dma((chunks,)),
            dma,
            dma,
            dma((2, dp)),
            dma((2, dp)),
            dma((3,)),
            dma((3,)),
            dma((chunks,)),
            dma((chunks,)),
            dma((2, dp)),
            dma((2, dp)),
        ],
        compiler_params=pltpu.CompilerParams(
            collective_id=0, has_side_effects=True, vmem_limit_bytes=used + 8 * 2**20
        ),
    )(
        *[
            pltpu.with_memory_space_constraint(array, pltpu.HBM)
            for array in (
                segment_adapter,
                slot_per_adapter,
                normed_layer_input,
                key_value_gradient,
                key_value_weight,
                adapter_down_weight.reshape(held, feats),
                adapter_up_weight.reshape(held, cols),
            )
        ],
    )
    grad_input, grad_down, grad_up = pl.pallas_call(
        write,
        out_shape=(
            jax.ShapeDtypeStruct((rows, feats), bf16),
            jax.ShapeDtypeStruct((held, feats), f32),
            jax.ShapeDtypeStruct((held, cols), f32),
        ),
        in_specs=[inside] * 3,
        out_specs=(anywhere,) * 3,
        scratch_shapes=[dma((3,))],
        compiler_params=pltpu.CompilerParams(vmem_limit_bytes=2**20),
    )(*[pltpu.with_memory_space_constraint(array, pltpu.VMEM) for array in made])
    return grad_input, grad_down.reshape(count, rank, feats), grad_up.reshape(count, rank, cols)


def solution(mesh):
    placed = (
        P(("groups", "dp"), "tensor"),
        P(("groups", "dp"), "tensor"),
        P(None, "tensor"),
        P("dp", None, "tensor"),
        P("dp", None, "tensor"),
        P(("groups", "dp")),
        P(),
    )
    return jax.shard_map(
        functools.partial(shards, mesh.shape["dp"]),
        mesh=mesh,
        in_specs=placed,
        out_specs=(
            P(("groups", "dp"), "tensor"),
            P(("groups", "dp"), None, "tensor"),
            P(("groups", "dp"), None, "tensor"),
        ),
        check_vma=False,
    )
```

```python
import functools
import math

import jax
import jax.numpy as jnp
from jax import lax
from jax.experimental import pallas as pl
from jax.experimental.pallas import tpu as pltpu
from jax.sharding import PartitionSpec as P

SEG = 128
MESH = pl.DeviceIdType.MESH
CHUNK = 256
EARLY = 2
FIRST = 4

adapter_scale = 2.0

NT = (((1,), (1,)), ((), ()))


def dot(a, b, dims=(((1,), (0,)), ((), ()))):
    return lax.dot_general(a, b, dims, preferred_element_type=jnp.float32)


def kernel(
    dp,
    rank,
    seg_hbm,
    slot_hbm,
    x_hbm,
    g_hbm,
    w_hbm,
    down_hbm,
    up_hbm,
    out,
    final_down,
    final_up,
    x,
    g,
    w_far,
    w_own,
    down,
    up,
    send,
    recv,
    acc,
    prod_in,
    prod_grad,
    low,
    low_mate,
    low_pair,
    low_peer,
    wide_grad,
    wide_in,
    rows_grad,
    dense_down,
    dense_up,
    send_down,
    send_up,
    recv_down,
    recv_up,
    seg_ref,
    slot_ref,
    load_sem,
    g_send,
    g_recv,
    far_send,
    far_recv,
    own_send,
    own_recv,
    map_send,
    map_recv,
    low_send,
    low_recv,
    chunk_send,
    chunk_recv,
    term_send,
    term_recv,
    ready_sem,
):
    t = lax.axis_index("tensor")
    me = lax.axis_index("dp")
    mate = t + 1 - 2 * lax.rem(t, 2)
    peer = lax.rem(t + 2, 4)
    cross = 3 - t
    rows, feats = x.shape
    chunks = feats // CHUNK
    segs = rows // SEG
    held = down.shape[0] // dp
    slots = down.shape[0] // rank
    blocks = down.shape[0] // 128

    def local(src, dst, sem):
        return pltpu.make_async_copy(src, dst, sem)

    def remote(src, dst, send_sem, recv_sem, **where):
        return pltpu.make_async_remote_copy(
            src_ref=src, dst_ref=dst, send_sem=send_sem, recv_sem=recv_sem, device_id=where, device_id_type=MESH
        )

    def held_rows(ref, index):
        return ref.at[pl.ds(pl.multiple_of(index * held, held), held)]

    def chunk_rows(ref, base, k):
        return ref.at[pl.ds(pl.multiple_of(base * feats + k * CHUNK, CHUNK), CHUNK)]

    loads = [
        local(g_hbm, g.at[0], load_sem.at[0]),
        local(w_hbm.at[pl.ds(pl.multiple_of(peer * feats, feats), feats)], w_far.at[0], load_sem.at[1]),
        local(x_hbm, x, load_sem.at[2]),
        local(down_hbm, held_rows(down, me), load_sem.at[3]),
        local(up_hbm, held_rows(up, me), load_sem.at[4]),
        local(w_hbm.at[pl.ds(pl.multiple_of(t * feats, feats), feats)], w_own.at[0], load_sem.at[5]),
        local(seg_hbm, seg_ref, load_sem.at[6]),
        local(slot_hbm, slot_ref, load_sem.at[7]),
    ]
    for load in loads:
        load.start()

    barrier = pltpu.get_barrier_semaphore()
    pl.semaphore_signal(barrier, inc=1, device_id={"tensor": mate}, device_id_type=MESH)
    pl.semaphore_signal(barrier, inc=1, device_id={"tensor": peer}, device_id_type=MESH)
    for d in range(1, dp):

        @pl.when(me + d < dp)
        def _():
            pl.semaphore_signal(barrier, inc=1, device_id={"dp": lax.rem(me + d, dp)}, device_id_type=MESH)

    pl.semaphore_wait(barrier, me + 2)
    for d in range(1, dp):

        @pl.when(me >= d)
        def _():
            pl.semaphore_signal(ready_sem, inc=1, device_id={"dp": lax.rem(me + dp - d, dp)}, device_id_type=MESH)

    copy_g = remote(g_hbm, g.at[1], g_send, g_recv, tensor=mate)
    copy_g.start()

    def copy_far(k):
        return remote(
            chunk_rows(w_hbm, cross, k), chunk_rows(w_far.at[1], 0, k), far_send.at[k], far_recv.at[k], tensor=mate
        )

    for k in range(chunks):
        copy_far(k).start()
    maps = []
    for d in range(1, dp):
        target = lax.rem(me + d, dp)
        maps.append(remote(up_hbm, held_rows(up, me), map_send.at[0, d], map_recv.at[0, d], dp=target))
        maps.append(remote(down_hbm, held_rows(down, me), map_send.at[1, d], map_recv.at[1, d], dp=target))
    copy_own = remote(
        w_hbm.at[pl.ds(pl.multiple_of(mate * feats, feats), feats)], w_own.at[1], own_send, own_recv, tensor=mate
    )
    copy_own.start()

    def copy_chunk(k):
        return remote(send.at[k], recv.at[k], chunk_send.at[k], chunk_recv.at[k], tensor=peer)

    def send_chunk(k, carry):
        copy_far(k).wait_recv()
        at = pl.ds(pl.multiple_of(k * CHUNK, CHUNK), CHUNK)
        part = dot(g[0], w_far[0, at, :], NT) + dot(g[1], w_far[1, at, :], NT)
        send[k] = part.astype(jnp.bfloat16)
        copy_chunk(k).start()
        return carry

    loads[0].wait()
    loads[1].wait()
    copy_g.wait_recv()
    lax.fori_loop(0, EARLY, send_chunk, 0)

    @pl.when(me < dp - 1)
    def _():
        pl.semaphore_wait(ready_sem, dp - 1 - me)

    loads[3].wait()
    loads[4].wait()
    for copy in maps:
        copy.start()
    lax.fori_loop(EARLY, FIRST, send_chunk, 0)

    for load in loads[2:3] + loads[6:8]:
        load.wait()
    for copy in maps:
        copy.wait_recv()

    def project(b, carry):
        at = pl.ds(pl.multiple_of(b * 128, 128), 128)
        prod_in[at, :] = dot(down[at, :], x[...], NT)
        prod_grad[at, :] = dot(up[at, :], g[0], NT)
        return carry

    lax.fori_loop(0, blocks, project, 0)
    chosen = []
    for s in range(segs):
        adapter = jnp.full((rank, SEG), seg_ref[s], jnp.int32)
        slot = jnp.zeros((rank, SEG), jnp.int32)
        for j in range(slots):
            slot = jnp.where(adapter == j, jnp.full((rank, SEG), slot_ref[j], jnp.int32), slot)
        chosen.append(slot)
    low[...] = jnp.zeros_like(low)

    def select(a, carry):
        at = pl.ds(pl.multiple_of(a * rank, rank), rank)
        for s in range(segs):
            span = slice(s * SEG, (s + 1) * SEG)
            low[0:rank, span] = jnp.where(chosen[s] == a, prod_in[at, span], low[0:rank, span])
            low[rank : 2 * rank, span] = jnp.where(chosen[s] == a, prod_grad[at, span], low[rank : 2 * rank, span])
        return carry

    lax.fori_loop(0, slots, select, 0)
    copy_low = remote(low, low_mate, low_send.at[0], low_recv.at[0], tensor=mate)
    copy_low.start()
    copy_low.wait_recv()
    low_pair[...] = low[...] + low_mate[...]
    half = pl.ds(pl.multiple_of(lax.rem(t, 2) * rank, rank), rank)
    copy_pair = remote(low_pair.at[half], low_peer.at[half], low_send.at[1], low_recv.at[1], tensor=peer)
    copy_pair.start()

    lax.fori_loop(FIRST, chunks, send_chunk, 0)

    loads[5].wait()
    copy_own.wait_recv()

    def own_chunk(k, carry):
        at = pl.ds(pl.multiple_of(k * CHUNK, CHUNK), CHUNK)
        acc[k] = dot(g[0], w_own[0, at, :], NT) + dot(g[1], w_own[1, at, :], NT)
        return carry

    lax.fori_loop(0, chunks, own_chunk, 0)

    copy_pair.wait_recv()
    copy_half = remote(low_peer.at[half], low_peer.at[half], low_send.at[2], low_recv.at[2], tensor=mate)
    copy_half.start()
    copy_half.wait_recv()
    scaled = (adapter_scale * (low_pair[...] + low_peer[...])).astype(jnp.bfloat16).astype(jnp.float32)

    def widen(a, carry):
        at = pl.ds(pl.multiple_of(a * rank, rank), rank)
        for s in range(segs):
            span = slice(s * SEG, (s + 1) * SEG)
            wide_in[at, span] = jnp.where(chosen[s] == a, scaled[0:rank, span], 0.0)
            wide_grad[at, span] = jnp.where(chosen[s] == a, scaled[rank : 2 * rank, span], 0.0)
        return carry

    lax.fori_loop(0, slots, widen, 0)

    def terms(b, carry):
        at = pl.ds(pl.multiple_of(b * 128, 128), 128)
        left = wide_grad[at, :].astype(jnp.bfloat16)
        for n in range(feats // 512):
            span = slice(n * 512, (n + 1) * 512)
            value = dot(left, x[:, span])
            dense_down[at, span] = value
            send_down[at, span] = value.astype(jnp.bfloat16)
        value = dot(wide_in[at, :].astype(jnp.bfloat16), g[0])
        dense_up[at, :] = value
        send_up[at, :] = value.astype(jnp.bfloat16)
        return carry

    lax.fori_loop(0, blocks, terms, 0)
    copies = []
    for d in range(1, dp):
        target = lax.rem(me + d, dp)
        copies.append(
            remote(held_rows(send_down, target), recv_down.at[d], term_send.at[0, d], term_recv.at[0, d], dp=target)
        )
        copies.append(
            remote(held_rows(send_up, target), recv_up.at[d], term_send.at[1, d], term_recv.at[1, d], dp=target)
        )
    for copy in copies:
        copy.start()

    for b in range(blocks):
        span = slice(b * 128, (b + 1) * 128)
        rows_grad[:, span] = wide_grad[span, :].T.astype(jnp.bfloat16)

    for k in range(chunks):
        acc[k] = acc[k] + dot(rows_grad[...], down[:, k * CHUNK : (k + 1) * CHUNK])

    def finish(k):
        copy_chunk(k).wait_recv()
        out[:, k * CHUNK : (k + 1) * CHUNK] = (acc[k] + recv[k].astype(jnp.float32)).astype(jnp.bfloat16)

    for k in range(chunks - 1):
        finish(k)

    for copy in copies:
        copy.wait_recv()
    mine = pl.ds(pl.multiple_of(me * held, held), held)
    final_down[...] = dense_down[mine, :]
    final_up[...] = dense_up[mine, :]
    for d in range(1, dp):
        final_down[...] += recv_down[d].astype(jnp.float32)
        final_up[...] += recv_up[d].astype(jnp.float32)

    copy_g.wait_send()
    copy_own.wait_send()
    copy_low.wait_send()
    copy_pair.wait_send()
    copy_half.wait_send()
    for k in range(chunks):
        copy_far(k).wait_send()
    for k in range(chunks):
        copy_chunk(k).wait_send()
    for copy in maps + copies:
        copy.wait_send()
    finish(chunks - 1)


def write(out, grad_down, grad_up, out_hbm, grad_down_hbm, grad_up_hbm, sem):
    copies = [
        pltpu.make_async_copy(out, out_hbm, sem.at[0]),
        pltpu.make_async_copy(grad_down, grad_down_hbm, sem.at[1]),
        pltpu.make_async_copy(grad_up, grad_up_hbm, sem.at[2]),
    ]
    for copy in copies:
        copy.start()
    for copy in copies:
        copy.wait()


def shards(
    dp,
    normed_layer_input,
    key_value_gradient,
    key_value_weight,
    adapter_down_weight,
    adapter_up_weight,
    segment_adapter,
    slot_per_adapter,
):
    rows, feats = normed_layer_input.shape
    cols = key_value_gradient.shape[1]
    count, rank, _ = adapter_down_weight.shape
    held = count * rank
    wide = dp * held
    chunks = feats // CHUNK
    bf16, f32 = jnp.bfloat16, jnp.float32
    vmem, dma = pltpu.VMEM, pltpu.SemaphoreType.DMA
    anywhere = pl.BlockSpec(memory_space=pl.ANY)
    buffers = [
        vmem((rows, feats), bf16),
        vmem((2, rows, cols), bf16),
        vmem((2, feats, cols), bf16),
        vmem((2, feats, cols), bf16),
        vmem((wide, feats), bf16),
        vmem((wide, cols), bf16),
        vmem((chunks, rows, CHUNK), bf16),
        vmem((chunks, rows, CHUNK), bf16),
        vmem((chunks, rows, CHUNK), f32),
        vmem((wide, rows), f32),
        vmem((wide, rows), f32),
        vmem((2 * rank, rows), f32),
        vmem((2 * rank, rows), f32),
        vmem((2 * rank, rows), f32),
        vmem((2 * rank, rows), f32),
        vmem((wide, rows), f32),
        vmem((wide, rows), f32),
        vmem((rows, wide), bf16),
        vmem((wide, feats), f32),
        vmem((wide, cols), f32),
        vmem((wide, feats), bf16),
        vmem((wide, cols), bf16),
        vmem((dp, held, feats), bf16),
        vmem((dp, held, cols), bf16),
    ]
    used = sum(math.prod(buffer.shape) * jnp.dtype(buffer.dtype).itemsize for buffer in buffers)
    inside = pl.BlockSpec(memory_space=pltpu.VMEM)
    made = pl.pallas_call(
        functools.partial(kernel, dp, rank),
        out_shape=(vmem((rows, feats), bf16), vmem((held, feats), f32), vmem((held, cols), f32)),
        in_specs=[anywhere] * 7,
        out_specs=(inside,) * 3,
        scratch_shapes=buffers
        + [
            pltpu.SMEM(segment_adapter.shape, jnp.int32),
            pltpu.SMEM(slot_per_adapter.shape, jnp.int32),
            dma((8,)),
            dma,
            dma,
            dma((chunks,)),
            dma((chunks,)),
            dma,
            dma,
            dma((2, dp)),
            dma((2, dp)),
            dma((3,)),
            dma((3,)),
            dma((chunks,)),
            dma((chunks,)),
            dma((2, dp)),
            dma((2, dp)),
            pltpu.SemaphoreType.REGULAR,
        ],
        compiler_params=pltpu.CompilerParams(
            collective_id=0, has_side_effects=True, vmem_limit_bytes=used + 8 * 2**20
        ),
    )(
        *[
            pltpu.with_memory_space_constraint(array, pltpu.HBM)
            for array in (
                segment_adapter,
                slot_per_adapter,
                normed_layer_input,
                key_value_gradient,
                key_value_weight,
                adapter_down_weight.reshape(held, feats),
                adapter_up_weight.reshape(held, cols),
            )
        ],
    )
    grad_input, grad_down, grad_up = pl.pallas_call(
        write,
        out_shape=(
            jax.ShapeDtypeStruct((rows, feats), bf16),
            jax.ShapeDtypeStruct((held, feats), f32),
            jax.ShapeDtypeStruct((held, cols), f32),
        ),
        in_specs=[inside] * 3,
        out_specs=(anywhere,) * 3,
        scratch_shapes=[dma((3,))],
        compiler_params=pltpu.CompilerParams(vmem_limit_bytes=2**20),
    )(*[pltpu.with_memory_space_constraint(array, pltpu.VMEM) for array in made])
    return grad_input, grad_down.reshape(count, rank, feats), grad_up.reshape(count, rank, cols)


def solution(mesh):
    placed = (
        P(("groups", "dp"), "tensor"),
        P(("groups", "dp"), "tensor"),
        P(None, "tensor"),
        P("dp", None, "tensor"),
        P("dp", None, "tensor"),
        P(("groups", "dp")),
        P(),
    )
    return jax.shard_map(
        functools.partial(shards, mesh.shape["dp"]),
        mesh=mesh,
        in_specs=placed,
        out_specs=(
            P(("groups", "dp"), "tensor"),
            P(("groups", "dp"), None, "tensor"),
            P(("groups", "dp"), None, "tensor"),
        ),
        check_vma=False,
    )
```
